512 devices in a mesh: shard: 128 (over y, x_lo, z), comp: 2 (over core), band: 2 (over x_hi).
Axes of the slice: x: 4 (x_hi: 2, x_lo: 2; x = x_hi * 2 + x_lo), y: 8, z: 8, core: 2. Of those that a mesh axis runs over, the one named last changes fastest.
Arguments:
- coefficients: float32 [2, 256, 5120], P(None, None, 'shard'), may hold values from -6 to 6
- pair_orders: int32 [128], replicated, may hold values from 1 to 2559, as said below
- legendre: bfloat16 [128, 5120, 512], P('shard', 'band', 'comp'), may hold values from -0.0048828125 to 0.0048828125
- derivative: bfloat16 [2, 128, 5120, 512], P('comp', 'shard', 'band'), may hold values from -0.0048828125 to 0.0048828125
Outputs:
- gradients: float32 [512, 6, 21600], P(('shard', 'band'), 'comp')
The draws below stay inside these ranges and needn't reach their ends.
Inputs may be any that keep to these rules, and one draw needn't show every extreme that they name: `pair_orders`: distinct values; the smallest and the largest allowed value both occur.
All inputs are finite; a program needn't handle non-finite values.
Results may differ from the reference program's by a relative error of at most 0.0032.
Values may be sent and summed in bfloat16 or wider, within the bound.
No kernel may reach another device: no remote copies, remote signals or barrier semaphores. Data moves between devices by JAX's collectives and lax.ppermute only.
A program may use at most 64 MiB of HBM per device.

```python
import jax
import jax.numpy as jnp
from jax import lax

DEGS = 5120
NLON = 21600
PAIRS = 128
ORD = 256
CYCLES = 512


def draw_pair_orders(key, part):
    key = jax.random.fold_in(key, 11)
    middle = jax.random.permutation(key, DEGS // 2 - 3)[:PAIRS - 2].astype(jnp.int32) + 2
    ends = jnp.array([1, DEGS // 2 - 1], dtype=jnp.int32)
    values = jnp.concatenate([ends, middle])
    placing = jax.random.permutation(jax.random.fold_in(key, 5), PAIRS)
    return values[placing]


def steps_of(key, dims, shards, smallest, top_value):
    def one(position, blocks):
        steps = jax.random.uniform(jax.random.fold_in(jax.random.fold_in(key, 6), position), (blocks,), jnp.float32, smallest / len(shards), top_value / len(shards))
        return jnp.repeat(jnp.exp(steps), dims[position] // blocks).reshape((-1,) + (1,) * (len(dims) - position - 1))

    level = one(*shards[0])
    for cut in shards[1:]:
        level = level * one(*cut)
    return level


def gaussian(stream_key, extent, scale, reach, split=(), kind=jnp.bfloat16):
    drawn = jax.random.normal(stream_key, extent, jnp.float32) * scale
    if len(split) > 0:
        drawn = steps_of(stream_key, extent, split, -0.22, 0.18) * drawn
    return jnp.clip(drawn, min=-reach, max=reach).astype(kind)


def setup_inputs(seed: int = 0) -> dict:
    seeds = jax.random.split(jax.random.key(seed), 5)
    coefficients = gaussian(seeds[0], (2, ORD, DEGS), 1.0, 6.0, ((2, 128),), jnp.float32)
    pair_orders = draw_pair_orders(jax.random.fold_in(seeds[4], 71), 0)
    legendre = gaussian(seeds[2], (PAIRS, DEGS, CYCLES), (DEGS * ORD) ** -0.5, 0.0048828125, ((0, 128), (1, 2), (2, 2)))
    derivative = gaussian(seeds[3], (2, PAIRS, DEGS, CYCLES), (DEGS * ORD) ** -0.5, 0.0048828125, ((0, 2), (1, 128), (2, 2)))
    return {"coefficients": coefficients, "pair_orders": pair_orders, "legendre": legendre, "derivative": derivative}


def cycle_angles(cycle_ids, total):
    return jnp.pi / 4.0 + (cycle_ids.astype(jnp.float32) + 0.5) * (jnp.pi / (2.0 * total))


def order_factors(order_values, sine_values):
    return (order_values.astype(jnp.float32) / DEGS) / sine_values[..., None]


def degree_weights(degree):
    linear_weight = (degree + 1.0) / DEGS
    shifted_weight = (degree + 2.0) / DEGS
    return linear_weight * shifted_weight, linear_weight, shifted_weight


def pack_pair(first_order, second_order, order_value, positions):
    item_count = positions.shape[0]
    split_point = DEGS - order_value
    padded = jnp.concatenate([first_order, jnp.zeros_like(first_order)], axis=1)
    shifted = lax.dynamic_slice_in_dim(padded, order_value + positions[0], item_count, 1)
    second_part = lax.dynamic_slice_in_dim(second_order, positions[0], item_count, 1)
    inside = positions < split_point
    lead_part = jnp.where(inside[None, :], shifted, 0.0)
    tail_part = jnp.where(inside[None, :], 0.0, second_part)
    degree = jnp.where(inside, positions + order_value, positions).astype(jnp.float32)
    return lead_part, tail_part, degree


def weighted(lead_part, tail_part, bases):
    both_orders = jnp.stack([lead_part, tail_part], axis=-1)
    scaled_parts = [factor[..., None, :, None] * both_orders for factor in bases]
    stacked = jnp.stack(scaled_parts, axis=-4)
    reordered = jnp.moveaxis(stacked, -2, -4)
    return reordered.reshape(reordered.shape[:-3] + (6, 2)).astype(jnp.bfloat16)


def components(basis_sums, group_zero, cotangent, order_factor):
    zero_cos = basis_sums[..., 0, 0, :]
    zero_sin = basis_sums[..., 0, 1, :]
    one_cos = basis_sums[..., 1, 0, :]
    one_sin = basis_sums[..., 1, 1, :]
    two_cos = basis_sums[..., 2, 0, :]
    two_sin = basis_sums[..., 2, 1, :]
    along_cos = two_cos - one_cos
    along_sin = two_sin - one_sin
    first_set = [along_cos, along_sin, -along_cos - zero_cos, -along_sin - zero_sin, zero_cos, zero_sin]
    second_set = [one_cos + cotangent * zero_cos, one_sin + cotangent * zero_sin,
                  order_factor * zero_sin, -(order_factor * zero_cos),
                  order_factor * two_sin, -(order_factor * two_cos)]
    chosen = [jnp.where(group_zero, left, right) for left, right in zip(first_set, second_set)]
    return jnp.stack(chosen, axis=-2)


def reference(coefficients, pair_orders, legendre, derivative):
    positions = jnp.arange(DEGS, dtype=jnp.int32)
    colatitude = cycle_angles(jnp.arange(CYCLES, dtype=jnp.int32), CYCLES)
    sine_values = jnp.sin(colatitude)
    cotangent = jnp.cos(colatitude) / sine_values

    def one_pair(pair_index):
        order_value = pair_orders[pair_index]
        first_order = lax.dynamic_index_in_dim(coefficients, 2 * pair_index, 1, keepdims=False)
        second_order = lax.dynamic_index_in_dim(coefficients, 2 * pair_index + 1, 1, keepdims=False)
        lead_part, tail_part, degree = pack_pair(first_order, second_order, order_value, positions)
        square_weight, linear_weight, shifted_weight = degree_weights(degree)
        zero_weights = jnp.zeros_like(degree)
        unit_weights = jnp.ones_like(degree)
        table_a = lax.dynamic_index_in_dim(legendre, pair_index, 0, keepdims=False).astype(jnp.float32)
        order_pair = jnp.stack([order_value, DEGS - order_value])
        order_factor = order_factors(order_pair, sine_values)
        results = []
        settings = ((0, (square_weight, linear_weight, zero_weights), (zero_weights, zero_weights, unit_weights)),
                    (1, (shifted_weight, zero_weights, zero_weights), (zero_weights, shifted_weight, unit_weights)))
        for group_index, a_bases, t_bases in settings:
            table_t = lax.dynamic_index_in_dim(derivative[group_index], pair_index, 0, keepdims=False).astype(jnp.float32)
            right_a = weighted(lead_part, tail_part, a_bases).astype(jnp.float32)
            right_t = weighted(lead_part, tail_part, t_bases).astype(jnp.float32)
            basis_sums = jnp.einsum("dr,dcj->rcj", table_a, right_a) + jnp.einsum("dr,dcj->rcj", table_t, right_t)
            results.append(components(basis_sums.reshape(CYCLES, 3, 2, 2), group_index == 0, cotangent[:, None], order_factor))
        return jnp.stack(results, axis=1)

    spectra = lax.map(one_pair, jnp.arange(PAIRS, dtype=jnp.int32))
    spectra = spectra.reshape(PAIRS, CYCLES, 2, 3, 2, 2).transpose(1, 2, 3, 4, 0, 5).reshape(CYCLES * 6, 2 * ORD)
    order_all = jnp.stack([pair_orders, DEGS - pair_orders], axis=1).reshape(-1)
    longitudes = jnp.arange(NLON, dtype=jnp.int32)
    phases = (order_all[:, None] * longitudes[None, :]) % NLON
    lon_angle = phases.astype(jnp.float32) * (2.0 * jnp.pi / NLON)
    lon_table = jnp.concatenate([jnp.cos(lon_angle), jnp.sin(lon_angle)], axis=0)
    fields = jnp.dot(spectra, lon_table, precision=lax.Precision.HIGHEST, preferred_element_type=jnp.float32)
    return fields.reshape(CYCLES, 6, NLON)
```

```python
import functools

import jax
import jax.numpy as jnp
from jax import lax
from jax.experimental import pallas as pl
from jax.experimental.pallas import tpu as pltpu
from jax.sharding import PartitionSpec as P

DEGS = 5120
NLON = 21600
PAIRS = 128
CYCLES = 512
SPAN = 40
LANES = 128
COLS = DEGS // LANES
HALF = COLS // 2
INNER = 256
OUTER = -(-NLON // INNER)
TURNS = 88
F32 = jnp.float32
BF16 = jnp.bfloat16
VMEM = pl.BlockSpec(memory_space=pltpu.VMEM)
HBM = pl.BlockSpec(memory_space=pltpu.HBM)


def params(mib):
    return pltpu.CompilerParams(vmem_limit_bytes=mib * 2**20)


def iota(shape, axis):
    return lax.broadcasted_iota(jnp.int32, shape, axis)


def send_kernel(coef_ref, out_ref, lines_ref, sems):
    shard = lax.axis_index("shard")
    lines_ref[...] = jnp.zeros_like(lines_ref)
    copies = []
    for k in range(2):
        for g in range(0, SPAN, 8):
            start = pl.multiple_of(lax.rem(shard * SPAN + (64 * k + g), LANES), 8)
            copies.append(
                pltpu.make_async_copy(
                    coef_ref.at[k, pl.ds(g, 8), :], lines_ref.at[pl.ds(start, 8), :], sems.at[k, g // 8]
                )
            )
            copies[-1].start()
    for copy in copies:
        copy.wait()
    out_ref[...] = lines_ref[...].T


def turn(phase):
    rest = wrap(phase)
    half = rest * (jnp.pi / NLON)
    square = half * half
    sine = jnp.full_like(half, -1.0 / 39916800.0)
    for c in (1.0 / 362880.0, -1.0 / 5040.0, 1.0 / 120.0, -1.0 / 6.0, 1.0):
        sine = sine * square + c
    sine = sine * half
    cosine = jnp.full_like(half, 1.0 / 479001600.0)
    for c in (-1.0 / 3628800.0, 1.0 / 40320.0, -1.0 / 720.0, 1.0 / 24.0, -0.5, 1.0):
        cosine = cosine * square + c
    return 1.0 - 2.0 * sine * sine, 2.0 * sine * cosine


def wrap(phase):
    return phase - jnp.round(phase * (1.0 / NLON)) * NLON


def table_kernel(orders_ref, lon_ref, turns_ref, cycles_ref):
    low = orders_ref[...].astype(F32)
    for j in range(2):
        order = low if j == 0 else DEGS - low
        inner = iota((INNER, PAIRS), 0).astype(F32)
        cosine, sine = turn(inner * order)
        lon_ref[:, pl.ds(j * PAIRS, PAIRS)] = cosine.astype(BF16)
        lon_ref[:, pl.ds((2 + j) * PAIRS, PAIRS)] = sine.astype(BF16)
        outer = iota((TURNS, PAIRS), 0).astype(F32)
        cosine, sine = turn(wrap(outer * order) * INNER)
        turns_ref[pl.ds(0, TURNS), pl.ds(j * PAIRS, PAIRS)] = cosine
        turns_ref[pl.ds(TURNS, TURNS), pl.ds(j * PAIRS, PAIRS)] = sine
    offset = (iota((8, CYCLES), 1).astype(F32) + (0.5 - CYCLES / 2)) * (jnp.pi / (2 * CYCLES))
    square = offset * offset
    sine = jnp.full_like(offset, 1.0 / 40320.0)
    for c in (-1.0 / 720.0, 1.0 / 24.0, -0.5, 1.0):
        sine = sine * square + c
    cosine = jnp.full_like(offset, 1.0 / 362880.0)
    for c in (-1.0 / 5040.0, 1.0 / 120.0, -1.0 / 6.0, 1.0):
        cosine = cosine * square + c
    row = iota((8, CYCLES), 0)
    own = jnp.sum(jnp.where(iota((1, PAIRS), 1) == lax.axis_index("shard"), low, 0.0), axis=1, keepdims=True)
    factor = jnp.where((row & 1) == 0, own, DEGS - own) / DEGS
    factor = jnp.where(row < 6, factor, -factor)
    cycles_ref[pl.ds(0, 8), :] = jnp.where(row < 4, -cosine * offset, factor) / sine
    cycles_ref[pl.ds(8, 8), :] = jnp.broadcast_to(own, (8, CYCLES))


def pack_kernel(cycles_ref, got_ref, weight_ref, flat_ref):
    group_zero = lax.axis_index("comp") == 0
    band = lax.axis_index("band")
    order = jnp.max(cycles_ref[8:16, 0:LANES]).astype(jnp.int32)
    lane = iota((8, LANES), 1)
    row = iota((8, LANES), 0)
    upper = row < 4
    columns = [None] * COLS
    on_cos = (row & 2) == 0
    for w in range(DEGS // SPAN // 4):
        four = got_ref[pl.ds(8 * w, 8), :]
        moved = pltpu.roll(four, 64, 1)
        turned = [(pltpu.roll(four, 2 * a, 0) if a else four) for a in range(4)]
        turned_sin = [(pltpu.roll(moved, 2 * a, 0) if a else moved) for a in range(4)]
        mixed = [jnp.where(on_cos, turned[a], turned_sin[(a + 1) % 4]) for a in range(4)]
        for t in range(4):
            piece = jnp.where(upper, mixed[-t % 4], mixed[(2 - t) % 4])
            first = SPAN * (4 * w + t)
            for v in range(first // LANES, (first + SPAN - 1) // LANES + 1):
                if columns[v] is None:
                    columns[v] = piece
                else:
                    columns[v] = jnp.where(lane >= first - LANES * v, piece, columns[v])
    for v in range(COLS):
        flat_ref[v] = columns[v]
    flat_ref[pl.ds(COLS, HALF)] = jnp.zeros((HALF, 8, LANES), F32)
    chunk = order // LANES
    rest = order - chunk * LANES
    back = lax.rem(LANES - rest, LANES)
    second_order = (row & 1) == 1
    for v in range(HALF):
        low = pltpu.roll(flat_ref[HALF * band + chunk + v], back, 1)
        high = pltpu.roll(flat_ref[jnp.minimum(HALF * band + chunk + v + 1, COLS + HALF - 1)], back, 1)
        lead = jnp.where(lane < LANES - rest, low, high)
        tail = flat_ref[HALF * band + v]
        position = (HALF * band + v) * LANES + lane
        inside = position < DEGS - order
        value = jnp.where(inside == second_order, 0.0, jnp.where(second_order, tail, lead))
        degree = jnp.where(inside, position + order, position).astype(F32)
        linear = (degree + 1.0) / DEGS
        shifted = (degree + 2.0) / DEGS
        on_values = jnp.where(group_zero, jnp.where(upper, linear * shifted, linear), jnp.where(upper, shifted, 0.0))
        on_deriv = jnp.where(upper, jnp.where(group_zero, 0.0, shifted), 1.0)
        both = jnp.concatenate([on_values * value, on_deriv * value], axis=0)
        weight_ref[:, pl.ds(v * LANES, LANES)] = both.astype(BF16)


def sums_kernel(cycles_ref, weight_ref, own_ref, deriv_ref, other_ref, out_ref, spec_ref, turned_ref):
    group_zero = lax.axis_index("comp") == 0
    weights = weight_ref[...]
    from_own = jnp.dot(weights, own_ref[...], preferred_element_type=F32)
    from_deriv = jnp.dot(weights, deriv_ref[...], preferred_element_type=F32)
    from_other = jnp.dot(weights, other_ref[...], preferred_element_type=F32)
    from_values = jnp.concatenate(
        [jnp.where(group_zero, from_own, from_other), jnp.where(group_zero, from_other, from_own)], axis=1
    )
    zero = from_values[0:4]
    one = from_values[4:8] + from_deriv[8:12]
    two = from_deriv[12:16]
    cotangent = cycles_ref[0:4]
    factor = cycles_ref[4:8]
    along = two - one

    def crossed(x):
        return factor * jnp.concatenate([x[2:4], x[0:2]], axis=0)

    parts = (
        jnp.where(group_zero, along, one + cotangent * zero),
        jnp.where(group_zero, -along - zero, crossed(zero)),
        jnp.where(group_zero, zero, crossed(two)),
    )
    spec_ref[...] = jnp.zeros_like(spec_ref)
    for c in range(3):
        for part in range(4):
            spec_ref[pl.ds(8 * part + 2 * c, 1), :] = parts[c][part : part + 1]
    turned_ref[...] = spec_ref[...].T
    for b in range(2):
        even = turned_ref[pl.ds(2 * b, PAIRS, stride=4), :]
        odd = turned_ref[pl.ds(2 * b + 1, PAIRS, stride=4), :]
        out_ref[pl.ds(b * PAIRS, PAIRS), :] = even + pltpu.roll(odd, 1, 1)


def field_kernel(got_ref, lon_ref, turns_ref, out_ref, left_ref):
    summed = got_ref[pl.ds(0, PAIRS), :] + got_ref[pl.ds(PAIRS, PAIRS), :]
    rows = summed.T
    cos_part = jnp.concatenate([rows[0:8], rows[8:16]], axis=1)
    sin_part = jnp.concatenate([rows[16:24], rows[24:32]], axis=1)
    for n in range(0, TURNS, 2):
        halves = []
        for d in range(2):
            turn_cos = turns_ref[pl.ds(n + d, 1), :]
            turn_sin = turns_ref[pl.ds(TURNS + n + d, 1), :]
            halves.append(
                jnp.concatenate(
                    [cos_part * turn_cos + sin_part * turn_sin, sin_part * turn_cos - cos_part * turn_sin], axis=1
                )
            )
        left_ref[pl.ds(8 * n, 16), :] = jnp.concatenate(halves, axis=0).astype(BF16)
    lon = lon_ref[...]
    step = 8
    for n in range(0, TURNS, step):
        field = lax.dot_general(
            left_ref[pl.ds(8 * n, 8 * step), :], lon, (((1,), (1,)), ((), ())), preferred_element_type=F32
        )
        for d in range(step):
            start = (n + d) * INNER
            width = min(INNER, NLON - start)
            if width <= 0:
                continue
            for c in range(3):
                out_ref[c, :, pl.ds(start, width)] = field[8 * d + 2 * c : 8 * d + 2 * c + 2, :width]


def on_device(coefficients, pair_orders, legendre, derivative):
    sent = pl.pallas_call(
        send_kernel,
        out_shape=jax.ShapeDtypeStruct((2 * PAIRS, LANES), F32),
        in_specs=[HBM],
        out_specs=VMEM,
        scratch_shapes=[pltpu.VMEM((LANES, 2 * PAIRS), F32), pltpu.SemaphoreType.DMA((2, SPAN // 8))],
        compiler_params=params(60),
        name="send",
    )(coefficients.transpose(0, 2, 1))
    sent, own = lax.optimization_barrier((sent, legendre[0]))
    got = lax.all_to_all(sent.reshape(PAIRS, 2, LANES), "shard", split_axis=0, concat_axis=0, tiled=True)
    other = lax.ppermute(own, "comp", [(0, 1), (1, 0)])
    lon, turns, cycles = pl.pallas_call(
        table_kernel,
        out_shape=(
            jax.ShapeDtypeStruct((INNER, 4 * PAIRS), BF16),
            jax.ShapeDtypeStruct((2 * TURNS, 2 * PAIRS), F32),
            jax.ShapeDtypeStruct((16, CYCLES), F32),
        ),
        in_specs=[VMEM],
        out_specs=(VMEM, VMEM, VMEM),
        compiler_params=params(4),
        cost_estimate=pl.CostEstimate(flops=400_000_000, bytes_accessed=600_000, transcendentals=0),
        name="tables",
    )(pair_orders.reshape(1, PAIRS))
    weights = pl.pallas_call(
        pack_kernel,
        out_shape=jax.ShapeDtypeStruct((16, HALF * LANES), BF16),
        in_specs=[VMEM, VMEM],
        out_specs=VMEM,
        scratch_shapes=[pltpu.VMEM((COLS + HALF, 8, LANES), F32)],
        compiler_params=params(4),
        cost_estimate=pl.CostEstimate(flops=30_000_000_000, bytes_accessed=300_000, transcendentals=0),
        name="pack",
    )(cycles, got.reshape(2 * PAIRS, LANES))
    spectra = pl.pallas_call(
        sums_kernel,
        out_shape=jax.ShapeDtypeStruct((2 * PAIRS, LANES), F32),
        in_specs=[VMEM] * 5,
        out_specs=VMEM,
        scratch_shapes=[pltpu.VMEM((LANES, CYCLES), F32), pltpu.VMEM((CYCLES, LANES), F32)],
        compiler_params=params(8),
        name="sums",
    )(cycles, weights, own, derivative[0, 0], other)
    pieces = lax.all_to_all(
        spectra.reshape(2 * PAIRS, 1, LANES), ("band", "shard"), split_axis=0, concat_axis=0, tiled=True
    )
    fields = pl.pallas_call(
        field_kernel,
        out_shape=jax.ShapeDtypeStruct((3, 2, NLON), F32),
        in_specs=[VMEM, VMEM, VMEM],
        out_specs=VMEM,
        scratch_shapes=[pltpu.VMEM((8 * TURNS, 4 * PAIRS), BF16)],
        compiler_params=params(8),
        name="fields",
    )(pieces.reshape(2 * PAIRS, LANES), lon, turns)
    return fields.transpose(1, 0, 2)


def solution(mesh):
    placed = (
        P(None, None, "shard"),
        P(),
        P("shard", "band", "comp"),
        P("comp", "shard", "band", None),
    )
    return jax.shard_map(
        on_device,
        mesh=mesh,
        in_specs=placed,
        out_specs=P(("shard", "band"), "comp", None),
        check_vma=False,
    )
```

```python
import functools

import jax
import jax.numpy as jnp
from jax import lax
from jax.experimental import pallas as pl
from jax.experimental.pallas import tpu as pltpu
from jax.sharding import PartitionSpec as P

DEGS = 5120
NLON = 21600
PAIRS = 128
CYCLES = 512
SPAN = 40
LANES = 128
COLS = DEGS // LANES
HALF = COLS // 2
INNER = 256
OUTER = -(-NLON // INNER)
TURNS = 88
FIRST = 76
F32 = jnp.float32
BF16 = jnp.bfloat16
VMEM = pl.BlockSpec(memory_space=pltpu.VMEM)
HBM = pl.BlockSpec(memory_space=pltpu.HBM)


def params(mib):
    return pltpu.CompilerParams(vmem_limit_bytes=mib * 2**20)


def iota(shape, axis):
    return lax.broadcasted_iota(jnp.int32, shape, axis)


def send_kernel(coef_ref, out_ref, lines_ref, sems):
    shard = lax.axis_index("shard")
    lines_ref[...] = jnp.zeros_like(lines_ref)
    copies = []
    for k in range(2):
        for g in range(0, SPAN, 8):
            start = pl.multiple_of(lax.rem(shard * SPAN + (64 * k + g), LANES), 8)
            copies.append(
                pltpu.make_async_copy(
                    coef_ref.at[k, pl.ds(g, 8), :], lines_ref.at[pl.ds(start, 8), :], sems.at[k, g // 8]
                )
            )
            copies[-1].start()
    for copy in copies:
        copy.wait()
    rows = lines_ref[...].T
    out_ref[pl.ds(0, 2 * (PAIRS - FIRST)), :] = rows[2 * FIRST :]
    out_ref[pl.ds(2 * (PAIRS - FIRST), 2 * FIRST), :] = rows[: 2 * FIRST]


def turn(phase):
    rest = wrap(phase)
    half = rest * (jnp.pi / NLON)
    square = half * half
    sine = jnp.full_like(half, -1.0 / 39916800.0)
    for c in (1.0 / 362880.0, -1.0 / 5040.0, 1.0 / 120.0, -1.0 / 6.0, 1.0):
        sine = sine * square + c
    sine = sine * half
    cosine = jnp.full_like(half, 1.0 / 479001600.0)
    for c in (-1.0 / 3628800.0, 1.0 / 40320.0, -1.0 / 720.0, 1.0 / 24.0, -0.5, 1.0):
        cosine = cosine * square + c
    return 1.0 - 2.0 * sine * sine, 2.0 * sine * cosine


def wrap(phase):
    return phase - jnp.round(phase * (1.0 / NLON)) * NLON


def table_kernel(orders_ref, lon_ref, turns_ref, cycles_ref):
    low = orders_ref[...].astype(F32)
    for j in range(2):
        order = low if j == 0 else DEGS - low
        inner = iota((INNER, PAIRS), 0).astype(F32)
        cosine, sine = turn(inner * order)
        lon_ref[:, pl.ds(j * PAIRS, PAIRS)] = cosine.astype(BF16)
        lon_ref[:, pl.ds((2 + j) * PAIRS, PAIRS)] = sine.astype(BF16)
        outer = iota((TURNS, PAIRS), 0).astype(F32)
        cosine, sine = turn(wrap(outer * order) * INNER)
        turns_ref[pl.ds(0, TURNS), pl.ds(j * PAIRS, PAIRS)] = cosine
        turns_ref[pl.ds(TURNS, TURNS), pl.ds(j * PAIRS, PAIRS)] = sine
    offset = (iota((8, CYCLES), 1).astype(F32) + (0.5 - CYCLES / 2)) * (jnp.pi / (2 * CYCLES))
    square = offset * offset
    sine = jnp.full_like(offset, 1.0 / 40320.0)
    for c in (-1.0 / 720.0, 1.0 / 24.0, -0.5, 1.0):
        sine = sine * square + c
    cosine = jnp.full_like(offset, 1.0 / 362880.0)
    for c in (-1.0 / 5040.0, 1.0 / 120.0, -1.0 / 6.0, 1.0):
        cosine = cosine * square + c
    row = iota((8, CYCLES), 0)
    own = jnp.sum(jnp.where(iota((1, PAIRS), 1) == lax.axis_index("shard"), low, 0.0), axis=1, keepdims=True)
    factor = jnp.where((row & 1) == 0, own, DEGS - own) / DEGS
    factor = jnp.where(row < 6, factor, -factor)
    cycles_ref[pl.ds(0, 8), :] = jnp.where(row < 4, -cosine * offset, factor) / sine
    cycles_ref[pl.ds(8, 8), :] = jnp.broadcast_to(own, (8, CYCLES))


def pack_kernel(cycles_ref, got_ref, weight_ref, flat_ref):
    group_zero = lax.axis_index("comp") == 0
    band = lax.axis_index("band")
    order = jnp.max(cycles_ref[8:16, 0:LANES]).astype(jnp.int32)
    lane = iota((8, LANES), 1)
    row = iota((8, LANES), 0)
    upper = row < 4
    columns = [None] * COLS
    on_cos = (row & 2) == 0
    for w in range(DEGS // SPAN // 4):
        four = got_ref[pl.ds(2 * ((4 * w - FIRST) % PAIRS), 8), :]
        moved = pltpu.roll(four, 64, 1)
        turned = [(pltpu.roll(four, 2 * a, 0) if a else four) for a in range(4)]
        turned_sin = [(pltpu.roll(moved, 2 * a, 0) if a else moved) for a in range(4)]
        mixed = [jnp.where(on_cos, turned[a], turned_sin[(a + 1) % 4]) for a in range(4)]
        for t in range(4):
            piece = jnp.where(upper, mixed[-t % 4], mixed[(2 - t) % 4])
            first = SPAN * (4 * w + t)
            for v in range(first // LANES, (first + SPAN - 1) // LANES + 1):
                if columns[v] is None:
                    columns[v] = piece
                else:
                    columns[v] = jnp.where(lane >= first - LANES * v, piece, columns[v])
    for v in range(COLS):
        flat_ref[v] = columns[v]
    flat_ref[pl.ds(COLS, HALF)] = jnp.zeros((HALF, 8, LANES), F32)
    chunk = order // LANES
    rest = order - chunk * LANES
    back = lax.rem(LANES - rest, LANES)
    second_order = (row & 1) == 1
    for v in range(HALF):
        low = pltpu.roll(flat_ref[HALF * band + chunk + v], back, 1)
        high = pltpu.roll(flat_ref[jnp.minimum(HALF * band + chunk + v + 1, COLS + HALF - 1)], back, 1)
        lead = jnp.where(lane < LANES - rest, low, high)
        tail = flat_ref[HALF * band + v]
        position = (HALF * band + v) * LANES + lane
        inside = position < DEGS - order
        value = jnp.where(inside == second_order, 0.0, jnp.where(second_order, tail, lead))
        degree = jnp.where(inside, position + order, position).astype(F32)
        linear = (degree + 1.0) / DEGS
        shifted = (degree + 2.0) / DEGS
        on_values = jnp.where(group_zero, jnp.where(upper, linear * shifted, linear), jnp.where(upper, shifted, 0.0))
        on_deriv = jnp.where(upper, jnp.where(group_zero, 0.0, shifted), 1.0)
        both = jnp.concatenate([on_values * value, on_deriv * value], axis=0)
        weight_ref[:, pl.ds(v * LANES, LANES)] = both.astype(BF16)


def sums_kernel(cycles_ref, weight_ref, own_ref, deriv_ref, other_ref, out_ref, spec_ref, turned_ref):
    group_zero = lax.axis_index("comp") == 0
    weights = weight_ref[...]
    from_own = jnp.dot(weights, own_ref[...], preferred_element_type=F32)
    from_deriv = jnp.dot(weights, deriv_ref[...], preferred_element_type=F32)
    from_other = jnp.dot(weights, other_ref[...], preferred_element_type=F32)
    from_values = jnp.concatenate(
        [jnp.where(group_zero, from_own, from_other), jnp.where(group_zero, from_other, from_own)], axis=1
    )
    zero = from_values[0:4]
    one = from_values[4:8] + from_deriv[8:12]
    two = from_deriv[12:16]
    cotangent = cycles_ref[0:4]
    factor = cycles_ref[4:8]
    along = two - one

    def crossed(x):
        return factor * jnp.concatenate([x[2:4], x[0:2]], axis=0)

    parts = (
        jnp.where(group_zero, along, one + cotangent * zero),
        jnp.where(group_zero, -along - zero, crossed(zero)),
        jnp.where(group_zero, zero, crossed(two)),
    )
    spec_ref[...] = jnp.zeros_like(spec_ref)
    for c in range(3):
        for part in range(4):
            spec_ref[pl.ds(8 * part + 2 * c, 1), :] = parts[c][part : part + 1]
    turned_ref[...] = spec_ref[...].T
    for b in range(2):
        for first, count, place in ((FIRST, PAIRS - FIRST, 0), (0, FIRST, PAIRS - FIRST)):
            even = turned_ref[pl.ds(4 * first + 2 * b, count, stride=4), :]
            odd = turned_ref[pl.ds(4 * first + 2 * b + 1, count, stride=4), :]
            out_ref[pl.ds(b * PAIRS + place, count), :] = even + pltpu.roll(odd, 1, 1)


def field_kernel(got_ref, lon_ref, turns_ref, out_ref, left_ref):
    summed = got_ref[pl.ds(0, PAIRS), :] + got_ref[pl.ds(PAIRS, PAIRS), :]
    rows = pltpu.roll(summed.T, FIRST, 1)
    cos_part = jnp.concatenate([rows[0:8], rows[8:16]], axis=1)
    sin_part = jnp.concatenate([rows[16:24], rows[24:32]], axis=1)
    for n in range(0, TURNS, 2):
        halves = []
        for d in range(2):
            turn_cos = turns_ref[pl.ds(n + d, 1), :]
            turn_sin = turns_ref[pl.ds(TURNS + n + d, 1), :]
            halves.append(
                jnp.concatenate(
                    [cos_part * turn_cos + sin_part * turn_sin, sin_part * turn_cos - cos_part * turn_sin], axis=1
                )
            )
        left_ref[pl.ds(8 * n, 16), :] = jnp.concatenate(halves, axis=0).astype(BF16)
    lon = lon_ref[...]
    step = 8
    for n in range(0, TURNS, step):
        field = lax.dot_general(
            left_ref[pl.ds(8 * n, 8 * step), :], lon, (((1,), (1,)), ((), ())), preferred_element_type=F32
        )
        for d in range(step):
            start = (n + d) * INNER
            width = min(INNER, NLON - start)
            if width <= 0:
                continue
            for c in range(3):
                out_ref[c, :, pl.ds(start, width)] = field[8 * d + 2 * c : 8 * d + 2 * c + 2, :width]


def on_device(coefficients, pair_orders, legendre, derivative):
    sent = pl.pallas_call(
        send_kernel,
        out_shape=jax.ShapeDtypeStruct((2 * PAIRS, LANES), F32),
        in_specs=[HBM],
        out_specs=VMEM,
        scratch_shapes=[pltpu.VMEM((LANES, 2 * PAIRS), F32), pltpu.SemaphoreType.DMA((2, SPAN // 8))],
        compiler_params=params(60),
        name="send",
    )(coefficients.transpose(0, 2, 1))
    sent, own = lax.optimization_barrier((sent, legendre[0]))
    shards = [(FIRST + i) % PAIRS for i in range(PAIRS)]
    got = lax.all_to_all(
        sent.reshape(PAIRS, 2, LANES), "shard", 0, 0, axis_index_groups=[shards], tiled=True
    )
    other = lax.ppermute(own, "comp", [(0, 1), (1, 0)])
    lon, turns, cycles = pl.pallas_call(
        table_kernel,
        out_shape=(
            jax.ShapeDtypeStruct((INNER, 4 * PAIRS), BF16),
            jax.ShapeDtypeStruct((2 * TURNS, 2 * PAIRS), F32),
            jax.ShapeDtypeStruct((16, CYCLES), F32),
        ),
        in_specs=[VMEM],
        out_specs=(VMEM, VMEM, VMEM),
        compiler_params=params(4),
        cost_estimate=pl.CostEstimate(flops=400_000_000, bytes_accessed=600_000, transcendentals=0),
        name="tables",
    )(pair_orders.reshape(1, PAIRS))
    weights = pl.pallas_call(
        pack_kernel,
        out_shape=jax.ShapeDtypeStruct((16, HALF * LANES), BF16),
        in_specs=[VMEM, VMEM],
        out_specs=VMEM,
        scratch_shapes=[pltpu.VMEM((COLS + HALF, 8, LANES), F32)],
        compiler_params=params(4),
        cost_estimate=pl.CostEstimate(flops=30_000_000_000, bytes_accessed=300_000, transcendentals=0),
        name="pack",
    )(cycles, got.reshape(2 * PAIRS, LANES))
    spectra = pl.pallas_call(
        sums_kernel,
        out_shape=jax.ShapeDtypeStruct((2 * PAIRS, LANES), F32),
        in_specs=[VMEM] * 5,
        out_specs=VMEM,
        scratch_shapes=[pltpu.VMEM((LANES, CYCLES), F32), pltpu.VMEM((CYCLES, LANES), F32)],
        compiler_params=params(8),
        name="sums",
    )(cycles, weights, own, derivative[0, 0], other)
    pieces = lax.all_to_all(
        spectra.reshape(2 * PAIRS, 1, LANES), ("band", "shard"), 0, 0,
        axis_index_groups=[[PAIRS * b + s for b in range(2) for s in shards]], tiled=True,
    )
    fields = pl.pallas_call(
        field_kernel,
        out_shape=jax.ShapeDtypeStruct((3, 2, NLON), F32),
        in_specs=[VMEM, VMEM, VMEM],
        out_specs=VMEM,
        scratch_shapes=[pltpu.VMEM((8 * TURNS, 4 * PAIRS), BF16)],
        compiler_params=params(8),
        name="fields",
    )(pieces.reshape(2 * PAIRS, LANES), lon, turns)
    return fields.transpose(1, 0, 2)


def solution(mesh):
    placed = (
        P(None, None, "shard"),
        P(),
        P("shard", "band", "comp"),
        P("comp", "shard", "band", None),
    )
    return jax.shard_map(
        on_device,
        mesh=mesh,
        in_specs=placed,
        out_specs=P(("shard", "band"), "comp", None),
        check_vma=False,
    )
```

```python
import functools

import jax
import jax.numpy as jnp
from jax import lax
from jax.experimental import pallas as pl
from jax.experimental.pallas import tpu as pltpu
from jax.sharding import PartitionSpec as P

DEGS = 5120
NLON = 21600
PAIRS = 128
CYCLES = 512
SPAN = 40
LANES = 128
COLS = DEGS // LANES
HALF = COLS // 2
INNER = 256
OUTER = -(-NLON // INNER)
TURNS = 88
STEP = 22
FIRST = 76
F32 = jnp.float32
BF16 = jnp.bfloat16
VMEM = pl.BlockSpec(memory_space=pltpu.VMEM)
HBM = pl.BlockSpec(memory_space=pltpu.HBM)


def params(mib):
    return pltpu.CompilerParams(vmem_limit_bytes=mib * 2**20)


def iota(shape, axis):
    return lax.broadcasted_iota(jnp.int32, shape, axis)


def send_kernel(coef_ref, out_ref, lines_ref, sems):
    shard = lax.axis_index("shard")
    lines_ref[...] = jnp.zeros_like(lines_ref)
    copies = []
    for k in range(2):
        for g in range(0, SPAN, 8):
            start = pl.multiple_of(lax.rem(shard * SPAN + (64 * k + g), LANES), 8)
            copies.append(
                pltpu.make_async_copy(
                    coef_ref.at[k, pl.ds(g, 8), :], lines_ref.at[pl.ds(start, 8), :], sems.at[k, g // 8]
                )
            )
            copies[-1].start()
    for copy in copies:
        copy.wait()
    rows = lines_ref[...].T
    out_ref[pl.ds(0, 2 * (PAIRS - FIRST)), :] = rows[2 * FIRST :]
    out_ref[pl.ds(2 * (PAIRS - FIRST), 2 * FIRST), :] = rows[: 2 * FIRST]


def turn(phase):
    rest = wrap(phase)
    half = rest * (jnp.pi / NLON)
    square = half * half
    sine = jnp.full_like(half, -1.0 / 39916800.0)
    for c in (1.0 / 362880.0, -1.0 / 5040.0, 1.0 / 120.0, -1.0 / 6.0, 1.0):
        sine = sine * square + c
    sine = sine * half
    cosine = jnp.full_like(half, 1.0 / 479001600.0)
    for c in (-1.0 / 3628800.0, 1.0 / 40320.0, -1.0 / 720.0, 1.0 / 24.0, -0.5, 1.0):
        cosine = cosine * square + c
    return 1.0 - 2.0 * sine * sine, 2.0 * sine * cosine


def wrap(phase):
    return phase - jnp.round(phase * (1.0 / NLON)) * NLON


def table_kernel(orders_ref, lon_ref, turns_ref, cycles_ref):
    low = orders_ref[...].astype(F32)
    for j in range(2):
        order = low if j == 0 else DEGS - low
        inner = iota((INNER, PAIRS), 0).astype(F32)
        cosine, sine = turn(inner * order)
        lon_ref[:, pl.ds(j * PAIRS, PAIRS)] = cosine.astype(BF16)
        lon_ref[:, pl.ds((2 + j) * PAIRS, PAIRS)] = sine.astype(BF16)
        outer = iota((TURNS, PAIRS), 0).astype(F32)
        cosine, sine = turn(wrap(outer * order) * INNER)
        turns_ref[pl.ds(0, TURNS), pl.ds(j * PAIRS, PAIRS)] = cosine
        turns_ref[pl.ds(TURNS, TURNS), pl.ds(j * PAIRS, PAIRS)] = sine
    offset = (iota((8, CYCLES), 1).astype(F32) + (0.5 - CYCLES / 2)) * (jnp.pi / (2 * CYCLES))
    square = offset * offset
    sine = jnp.full_like(offset, 1.0 / 40320.0)
    for c in (-1.0 / 720.0, 1.0 / 24.0, -0.5, 1.0):
        sine = sine * square + c
    cosine = jnp.full_like(offset, 1.0 / 362880.0)
    for c in (-1.0 / 5040.0, 1.0 / 120.0, -1.0 / 6.0, 1.0):
        cosine = cosine * square + c
    row = iota((8, CYCLES), 0)
    own = jnp.sum(jnp.where(iota((1, PAIRS), 1) == lax.axis_index("shard"), low, 0.0), axis=1, keepdims=True)
    factor = jnp.where((row & 1) == 0, own, DEGS - own) / DEGS
    factor = jnp.where(row < 6, factor, -factor)
    cycles_ref[pl.ds(0, 8), :] = jnp.where(row < 4, -cosine * offset, factor) / sine
    cycles_ref[pl.ds(8, 8), :] = jnp.broadcast_to(own, (8, CYCLES))


def pack_kernel(cycles_ref, got_ref, weight_ref, flat_ref):
    group_zero = lax.axis_index("comp") == 0
    band = lax.axis_index("band")
    order = jnp.max(cycles_ref[8:16, 0:LANES]).astype(jnp.int32)
    lane = iota((8, LANES), 1)
    row = iota((8, LANES), 0)
    upper = row < 4
    columns = [None] * COLS
    on_cos = (row & 2) == 0
    for w in range(DEGS // SPAN // 4):
        four = got_ref[pl.ds(2 * ((4 * w - FIRST) % PAIRS), 8), :]
        moved = pltpu.roll(four, 64, 1)
        turned = [(pltpu.roll(four, 2 * a, 0) if a else four) for a in range(4)]
        turned_sin = [(pltpu.roll(moved, 2 * a, 0) if a else moved) for a in range(4)]
        mixed = [jnp.where(on_cos, turned[a], turned_sin[(a + 1) % 4]) for a in range(4)]
        for t in range(4):
            piece = jnp.where(upper, mixed[-t % 4], mixed[(2 - t) % 4])
            first = SPAN * (4 * w + t)
            for v in range(first // LANES, (first + SPAN - 1) // LANES + 1):
                if columns[v] is None:
                    columns[v] = piece
                else:
                    columns[v] = jnp.where(lane >= first - LANES * v, piece, columns[v])
    for v in range(COLS):
        flat_ref[v] = columns[v]
    flat_ref[pl.ds(COLS, HALF)] = jnp.zeros((HALF, 8, LANES), F32)
    chunk = order // LANES
    rest = order - chunk * LANES
    back = lax.rem(LANES - rest, LANES)
    second_order = (row & 1) == 1
    for v in range(HALF):
        low = pltpu.roll(flat_ref[HALF * band + chunk + v], back, 1)
        high = pltpu.roll(flat_ref[jnp.minimum(HALF * band + chunk + v + 1, COLS + HALF - 1)], back, 1)
        lead = jnp.where(lane < LANES - rest, low, high)
        tail = flat_ref[HALF * band + v]
        position = (HALF * band + v) * LANES + lane
        inside = position < DEGS - order
        value = jnp.where(inside == second_order, 0.0, jnp.where(second_order, tail, lead))
        degree = jnp.where(inside, position + order, position).astype(F32)
        linear = (degree + 1.0) / DEGS
        shifted = (degree + 2.0) / DEGS
        on_values = jnp.where(group_zero, jnp.where(upper, linear * shifted, linear), jnp.where(upper, shifted, 0.0))
        on_deriv = jnp.where(upper, jnp.where(group_zero, 0.0, shifted), 1.0)
        both = jnp.concatenate([on_values * value, on_deriv * value], axis=0)
        weight_ref[:, pl.ds(v * LANES, LANES)] = both.astype(BF16)


def sums_kernel(cycles_ref, weight_ref, own_ref, deriv_ref, other_ref, out_ref, spec_ref, turned_ref):
    group_zero = lax.axis_index("comp") == 0
    weights = weight_ref[...]
    from_own = jnp.dot(weights, own_ref[...], preferred_element_type=F32)
    from_deriv = jnp.dot(weights, deriv_ref[...], preferred_element_type=F32)
    from_other = jnp.dot(weights, other_ref[...], preferred_element_type=F32)
    from_values = jnp.concatenate(
        [jnp.where(group_zero, from_own, from_other), jnp.where(group_zero, from_other, from_own)], axis=1
    )
    zero = from_values[0:4]
    one = from_values[4:8] + from_deriv[8:12]
    two = from_deriv[12:16]
    cotangent = cycles_ref[0:4]
    factor = cycles_ref[4:8]
    along = two - one

    def crossed(x):
        return factor * jnp.concatenate([x[2:4], x[0:2]], axis=0)

    parts = (
        jnp.where(group_zero, along, one + cotangent * zero),
        jnp.where(group_zero, -along - zero, crossed(zero)),
        jnp.where(group_zero, zero, crossed(two)),
    )
    spec_ref[...] = jnp.zeros_like(spec_ref)
    for c in range(3):
        for part in range(4):
            spec_ref[pl.ds(8 * part + 2 * c, 1), :] = parts[c][part : part + 1]
    turned_ref[...] = spec_ref[...].T
    for b in range(2):
        for first, count, place in ((FIRST, PAIRS - FIRST, 0), (0, FIRST, PAIRS - FIRST)):
            even = turned_ref[pl.ds(4 * first + 2 * b, count, stride=4), :]
            odd = turned_ref[pl.ds(4 * first + 2 * b + 1, count, stride=4), :]
            out_ref[pl.ds(b * PAIRS + place, count), :] = even + pltpu.roll(odd, 1, 1)


def field_kernel(got_ref, lon_ref, turns_ref, out_ref, left_ref, *rest):
    parts, sems = rest[:-1], rest[-1]
    summed = got_ref[pl.ds(0, PAIRS), :] + got_ref[pl.ds(PAIRS, PAIRS), :]
    rows = pltpu.roll(summed.T, FIRST, 1)
    cos_part = jnp.concatenate([rows[0:8], rows[8:16]], axis=1)
    sin_part = jnp.concatenate([rows[16:24], rows[24:32]], axis=1)
    lon = lon_ref[...]
    copies = []
    for i, part_ref in enumerate(parts):
        first = STEP * i
        for n in range(first, first + STEP, 2):
            halves = []
            for d in range(2):
                turn_cos = turns_ref[pl.ds(n + d, 1), :]
                turn_sin = turns_ref[pl.ds(TURNS + n + d, 1), :]
                halves.append(
                    jnp.concatenate(
                        [cos_part * turn_cos + sin_part * turn_sin, sin_part * turn_cos - cos_part * turn_sin], axis=1
                    )
                )
            left_ref[pl.ds(8 * n, 16), :] = jnp.concatenate(halves, axis=0).astype(BF16)
        field = lax.dot_general(
            left_ref[pl.ds(8 * first, 8 * STEP), :], lon, (((1,), (1,)), ((), ())), preferred_element_type=F32
        )
        for d in range(STEP):
            width = min(INNER, NLON - (first + d) * INNER)
            if width <= 0:
                continue
            for c in range(3):
                part_ref[c, :, pl.ds(d * INNER, width)] = field[8 * d + 2 * c : 8 * d + 2 * c + 2, :width]
        width = part_ref.shape[2]
        copies.append(pltpu.make_async_copy(part_ref, out_ref.at[:, :, pl.ds(first * INNER, width)], sems.at[i]))
        copies[-1].start()
    for copy in copies:
        copy.wait()


def on_device(coefficients, pair_orders, legendre, derivative):
    sent = pl.pallas_call(
        send_kernel,
        out_shape=jax.ShapeDtypeStruct((2 * PAIRS, LANES), F32),
        in_specs=[HBM],
        out_specs=VMEM,
        scratch_shapes=[pltpu.VMEM((LANES, 2 * PAIRS), F32), pltpu.SemaphoreType.DMA((2, SPAN // 8))],
        compiler_params=params(60),
        name="send",
    )(coefficients.transpose(0, 2, 1))
    sent, own = lax.optimization_barrier((sent, legendre[0]))
    shards = [(FIRST + i) % PAIRS for i in range(PAIRS)]
    got = lax.all_to_all(
        sent.reshape(PAIRS, 2, LANES), "shard", 0, 0, axis_index_groups=[shards], tiled=True
    )
    other = lax.ppermute(own, "comp", [(0, 1), (1, 0)])
    lon, turns, cycles = pl.pallas_call(
        table_kernel,
        out_shape=(
            jax.ShapeDtypeStruct((INNER, 4 * PAIRS), BF16),
            jax.ShapeDtypeStruct((2 * TURNS, 2 * PAIRS), F32),
            jax.ShapeDtypeStruct((16, CYCLES), F32),
        ),
        in_specs=[VMEM],
        out_specs=(VMEM, VMEM, VMEM),
        compiler_params=params(4),
        cost_estimate=pl.CostEstimate(flops=400_000_000, bytes_accessed=600_000, transcendentals=0),
        name="tables",
    )(pair_orders.reshape(1, PAIRS))
    weights = pl.pallas_call(
        pack_kernel,
        out_shape=jax.ShapeDtypeStruct((16, HALF * LANES), BF16),
        in_specs=[VMEM, VMEM],
        out_specs=VMEM,
        scratch_shapes=[pltpu.VMEM((COLS + HALF, 8, LANES), F32)],
        compiler_params=params(4),
        cost_estimate=pl.CostEstimate(flops=30_000_000_000, bytes_accessed=300_000, transcendentals=0),
        name="pack",
    )(cycles, got.reshape(2 * PAIRS, LANES))
    spectra = pl.pallas_call(
        sums_kernel,
        out_shape=jax.ShapeDtypeStruct((2 * PAIRS, LANES), F32),
        in_specs=[VMEM] * 5,
        out_specs=VMEM,
        scratch_shapes=[pltpu.VMEM((LANES, CYCLES), F32), pltpu.VMEM((CYCLES, LANES), F32)],
        compiler_params=params(8),
        name="sums",
    )(cycles, weights, own, derivative[0, 0], other)
    pieces = lax.all_to_all(
        spectra.reshape(2 * PAIRS, 1, LANES), ("band", "shard"), 0, 0,
        axis_index_groups=[[PAIRS * b + s for b in range(2) for s in shards]], tiled=True,
    )
    fields = pl.pallas_call(
        field_kernel,
        out_shape=jax.ShapeDtypeStruct((3, 2, NLON), F32),
        in_specs=[VMEM, VMEM, VMEM],
        out_specs=HBM,
        scratch_shapes=[
            pltpu.VMEM((8 * TURNS, 4 * PAIRS), BF16),
            *[pltpu.VMEM((3, 2, min(STEP * INNER, NLON - n * INNER)), F32) for n in range(0, TURNS, STEP)],
            pltpu.SemaphoreType.DMA((TURNS // STEP,)),
        ],
        compiler_params=params(8),
        name="fields",
    )(pieces.reshape(2 * PAIRS, LANES), lon, turns)
    return fields.transpose(1, 0, 2)


def solution(mesh):
    placed = (
        P(None, None, "shard"),
        P(),
        P("shard", "band", "comp"),
        P("comp", "shard", "band", None),
    )
    return jax.shard_map(
        on_device,
        mesh=mesh,
        in_specs=placed,
        out_specs=P(("shard", "band"), "comp", None),
        check_vma=False,
    )
```

```python
import functools

import jax
import jax.numpy as jnp
from jax import lax
from jax.experimental import pallas as pl
from jax.experimental.pallas import tpu as pltpu
from jax.sharding import PartitionSpec as P

DEGS = 5120
NLON = 21600
PAIRS = 128
CYCLES = 512
SPAN = 40
LANES = 128
COLS = DEGS // LANES
HALF = COLS // 2
INNER = 256
OUTER = -(-NLON // INNER)
TURNS = 88
PARTS = 5
PART = HALF * LANES // PARTS
STEP = 22
FIRST = 76
F32 = jnp.float32
BF16 = jnp.bfloat16
VMEM = pl.BlockSpec(memory_space=pltpu.VMEM)
HBM = pl.BlockSpec(memory_space=pltpu.HBM)


def params(mib):
    return pltpu.CompilerParams(vmem_limit_bytes=mib * 2**20)


def iota(shape, axis):
    return lax.broadcasted_iota(jnp.int32, shape, axis)


def send_kernel(coef_ref, out_ref, lines_ref, sems):
    shard = lax.axis_index("shard")
    lines_ref[...] = jnp.zeros_like(lines_ref)
    copies = []
    for k in range(2):
        for g in range(0, SPAN, 8):
            start = pl.multiple_of(lax.rem(shard * SPAN + (64 * k + g), LANES), 8)
            copies.append(
                pltpu.make_async_copy(
                    coef_ref.at[k, pl.ds(g, 8), :], lines_ref.at[pl.ds(start, 8), :], sems.at[k, g // 8]
                )
            )
            copies[-1].start()
    for copy in copies:
        copy.wait()
    rows = lines_ref[...].T
    out_ref[pl.ds(0, 2 * (PAIRS - FIRST)), :] = rows[2 * FIRST :]
    out_ref[pl.ds(2 * (PAIRS - FIRST), 2 * FIRST), :] = rows[: 2 * FIRST]


def turn(phase):
    rest = wrap(phase)
    half = rest * (jnp.pi / NLON)
    square = half * half
    sine = jnp.full_like(half, -1.0 / 39916800.0)
    for c in (1.0 / 362880.0, -1.0 / 5040.0, 1.0 / 120.0, -1.0 / 6.0, 1.0):
        sine = sine * square + c
    sine = sine * half
    cosine = jnp.full_like(half, 1.0 / 479001600.0)
    for c in (-1.0 / 3628800.0, 1.0 / 40320.0, -1.0 / 720.0, 1.0 / 24.0, -0.5, 1.0):
        cosine = cosine * square + c
    return 1.0 - 2.0 * sine * sine, 2.0 * sine * cosine


def wrap(phase):
    return phase - jnp.round(phase * (1.0 / NLON)) * NLON


def table_kernel(orders_ref, lon_ref, turns_ref, cycles_ref):
    low = orders_ref[...].astype(F32)
    for j in range(2):
        order = low if j == 0 else DEGS - low
        inner = iota((INNER, PAIRS), 0).astype(F32)
        cosine, sine = turn(inner * order)
        lon_ref[:, pl.ds(j * PAIRS, PAIRS)] = cosine.astype(BF16)
        lon_ref[:, pl.ds((2 + j) * PAIRS, PAIRS)] = sine.astype(BF16)
        outer = iota((TURNS, PAIRS), 0).astype(F32)
        cosine, sine = turn(wrap(outer * order) * INNER)
        turns_ref[pl.ds(0, TURNS), pl.ds(j * PAIRS, PAIRS)] = cosine
        turns_ref[pl.ds(TURNS, TURNS), pl.ds(j * PAIRS, PAIRS)] = sine
    offset = (iota((8, CYCLES), 1).astype(F32) + (0.5 - CYCLES / 2)) * (jnp.pi / (2 * CYCLES))
    square = offset * offset
    sine = jnp.full_like(offset, 1.0 / 40320.0)
    for c in (-1.0 / 720.0, 1.0 / 24.0, -0.5, 1.0):
        sine = sine * square + c
    cosine = jnp.full_like(offset, 1.0 / 362880.0)
    for c in (-1.0 / 5040.0, 1.0 / 120.0, -1.0 / 6.0, 1.0):
        cosine = cosine * square + c
    row = iota((8, CYCLES), 0)
    own = jnp.sum(jnp.where(iota((1, PAIRS), 1) == lax.axis_index("shard"), low, 0.0), axis=1, keepdims=True)
    factor = jnp.where((row & 1) == 0, own, DEGS - own) / DEGS
    factor = jnp.where(row < 6, factor, -factor)
    cycles_ref[pl.ds(0, 8), :] = jnp.where(row < 4, -cosine * offset, factor) / sine
    cycles_ref[pl.ds(8, 8), :] = jnp.broadcast_to(own, (8, CYCLES))


def pack_kernel(cycles_ref, got_ref, own_any, deriv_any, weight_ref, near_ref, flat_ref, own_ref, deriv_ref, sems):
    copies = []
    for c in range(PARTS):
        rows = pl.ds(c * PART, PART)
        copies.append(
            (
                pltpu.make_async_copy(own_any.at[rows, :], own_ref.at[rows, :], sems.at[0, c]),
                pltpu.make_async_copy(deriv_any.at[rows, :], deriv_ref.at[rows, :], sems.at[1, c]),
            )
        )
        for copy in copies[-1]:
            copy.start()
    group_zero = lax.axis_index("comp") == 0
    band = lax.axis_index("band")
    order = jnp.max(cycles_ref[8:16, 0:LANES]).astype(jnp.int32)
    lane = iota((8, LANES), 1)
    row = iota((8, LANES), 0)
    upper = row < 4
    columns = [None] * COLS
    on_cos = (row & 2) == 0
    for w in range(DEGS // SPAN // 4):
        four = got_ref[pl.ds(2 * ((4 * w - FIRST) % PAIRS), 8), :]
        moved = pltpu.roll(four, 64, 1)
        turned = [(pltpu.roll(four, 2 * a, 0) if a else four) for a in range(4)]
        turned_sin = [(pltpu.roll(moved, 2 * a, 0) if a else moved) for a in range(4)]
        mixed = [jnp.where(on_cos, turned[a], turned_sin[(a + 1) % 4]) for a in range(4)]
        for t in range(4):
            piece = jnp.where(upper, mixed[-t % 4], mixed[(2 - t) % 4])
            first = SPAN * (4 * w + t)
            for v in range(first // LANES, (first + SPAN - 1) // LANES + 1):
                if columns[v] is None:
                    columns[v] = piece
                else:
                    columns[v] = jnp.where(lane >= first - LANES * v, piece, columns[v])
    for v in range(COLS):
        flat_ref[v] = columns[v]
    flat_ref[pl.ds(COLS, HALF)] = jnp.zeros((HALF, 8, LANES), F32)
    chunk = order // LANES
    rest = order - chunk * LANES
    back = lax.rem(LANES - rest, LANES)
    second_order = (row & 1) == 1
    for v in range(HALF):
        low = pltpu.roll(flat_ref[HALF * band + chunk + v], back, 1)
        high = pltpu.roll(flat_ref[jnp.minimum(HALF * band + chunk + v + 1, COLS + HALF - 1)], back, 1)
        lead = jnp.where(lane < LANES - rest, low, high)
        tail = flat_ref[HALF * band + v]
        position = (HALF * band + v) * LANES + lane
        inside = position < DEGS - order
        value = jnp.where(inside == second_order, 0.0, jnp.where(second_order, tail, lead))
        degree = jnp.where(inside, position + order, position).astype(F32)
        linear = (degree + 1.0) / DEGS
        shifted = (degree + 2.0) / DEGS
        on_values = jnp.where(group_zero, jnp.where(upper, linear * shifted, linear), jnp.where(upper, shifted, 0.0))
        on_deriv = jnp.where(upper, jnp.where(group_zero, 0.0, shifted), 1.0)
        both = jnp.concatenate([on_values * value, on_deriv * value], axis=0)
        weight_ref[:, pl.ds(v * LANES, LANES)] = both.astype(BF16)
    from_own = jnp.zeros((16, CYCLES // 2), F32)
    from_deriv = jnp.zeros((16, CYCLES), F32)
    for c in range(PARTS):
        for copy in copies[c]:
            copy.wait()
        rows = pl.ds(c * PART, PART)
        weights = weight_ref[:, rows]
        from_own += jnp.dot(weights, own_ref[rows, :], preferred_element_type=F32)
        from_deriv += jnp.dot(weights, deriv_ref[rows, :], preferred_element_type=F32)
    near_ref[:, pl.ds(0, CYCLES // 2)] = from_own
    near_ref[:, pl.ds(CYCLES // 2, CYCLES)] = from_deriv


def sums_kernel(cycles_ref, weight_ref, near_ref, other_ref, out_ref, spec_ref, turned_ref):
    group_zero = lax.axis_index("comp") == 0
    from_own = near_ref[:, : CYCLES // 2]
    from_deriv = near_ref[:, CYCLES // 2 :]
    from_other = jnp.dot(weight_ref[...], other_ref[...], preferred_element_type=F32)
    from_values = jnp.concatenate(
        [jnp.where(group_zero, from_own, from_other), jnp.where(group_zero, from_other, from_own)], axis=1
    )
    zero = from_values[0:4]
    one = from_values[4:8] + from_deriv[8:12]
    two = from_deriv[12:16]
    cotangent = cycles_ref[0:4]
    factor = cycles_ref[4:8]
    along = two - one

    def crossed(x):
        return factor * jnp.concatenate([x[2:4], x[0:2]], axis=0)

    parts = (
        jnp.where(group_zero, along, one + cotangent * zero),
        jnp.where(group_zero, -along - zero, crossed(zero)),
        jnp.where(group_zero, zero, crossed(two)),
    )
    spec_ref[...] = jnp.zeros_like(spec_ref)
    for c in range(3):
        for part in range(4):
            spec_ref[pl.ds(8 * part + 2 * c, 1), :] = parts[c][part : part + 1]
    turned_ref[...] = spec_ref[...].T
    for b in range(2):
        for first, count, place in ((FIRST, PAIRS - FIRST, 0), (0, FIRST, PAIRS - FIRST)):
            even = turned_ref[pl.ds(4 * first + 2 * b, count, stride=4), :]
            odd = turned_ref[pl.ds(4 * first + 2 * b + 1, count, stride=4), :]
            out_ref[pl.ds(b * PAIRS + place, count), :] = even + pltpu.roll(odd, 1, 1)


def field_kernel(got_ref, lon_ref, turns_ref, out_ref, left_ref, *rest):
    parts, sems = rest[:-1], rest[-1]
    summed = got_ref[pl.ds(0, PAIRS), :] + got_ref[pl.ds(PAIRS, PAIRS), :]
    rows = pltpu.roll(summed.T, FIRST, 1)
    cos_part = jnp.concatenate([rows[0:8], rows[8:16]], axis=1)
    sin_part = jnp.concatenate([rows[16:24], rows[24:32]], axis=1)
    lon = lon_ref[...]
    copies = []
    for i, part_ref in enumerate(parts):
        first = STEP * i
        for n in range(first, first + STEP, 2):
            halves = []
            for d in range(2):
                turn_cos = turns_ref[pl.ds(n + d, 1), :]
                turn_sin = turns_ref[pl.ds(TURNS + n + d, 1), :]
                halves.append(
                    jnp.concatenate(
                        [cos_part * turn_cos + sin_part * turn_sin, sin_part * turn_cos - cos_part * turn_sin], axis=1
                    )
                )
            left_ref[pl.ds(8 * n, 16), :] = jnp.concatenate(halves, axis=0).astype(BF16)
        field = lax.dot_general(
            left_ref[pl.ds(8 * first, 8 * STEP), :], lon, (((1,), (1,)), ((), ())), preferred_element_type=F32
        )
        for d in range(STEP):
            width = min(INNER, NLON - (first + d) * INNER)
            if width <= 0:
                continue
            for c in range(3):
                part_ref[c, :, pl.ds(d * INNER, width)] = field[8 * d + 2 * c : 8 * d + 2 * c + 2, :width]
        width = part_ref.shape[2]
        copies.append(pltpu.make_async_copy(part_ref, out_ref.at[:, :, pl.ds(first * INNER, width)], sems.at[i]))
        copies[-1].start()
    for copy in copies:
        copy.wait()


def on_device(coefficients, pair_orders, legendre, derivative):
    sent = pl.pallas_call(
        send_kernel,
        out_shape=jax.ShapeDtypeStruct((2 * PAIRS, LANES), F32),
        in_specs=[HBM],
        out_specs=VMEM,
        scratch_shapes=[pltpu.VMEM((LANES, 2 * PAIRS), F32), pltpu.SemaphoreType.DMA((2, SPAN // 8))],
        compiler_params=params(60),
        name="send",
    )(coefficients.transpose(0, 2, 1))
    sent, own = lax.optimization_barrier((sent, legendre[0]))
    shards = [(FIRST + i) % PAIRS for i in range(PAIRS)]
    got = lax.all_to_all(
        sent.reshape(PAIRS, 2, LANES), "shard", 0, 0, axis_index_groups=[shards], tiled=True
    )
    other = lax.ppermute(own, "comp", [(0, 1), (1, 0)])
    lon, turns, cycles = pl.pallas_call(
        table_kernel,
        out_shape=(
            jax.ShapeDtypeStruct((INNER, 4 * PAIRS), BF16),
            jax.ShapeDtypeStruct((2 * TURNS, 2 * PAIRS), F32),
            jax.ShapeDtypeStruct((16, CYCLES), F32),
        ),
        in_specs=[VMEM],
        out_specs=(VMEM, VMEM, VMEM),
        compiler_params=params(4),
        cost_estimate=pl.CostEstimate(flops=400_000_000, bytes_accessed=600_000, transcendentals=0),
        name="tables",
    )(pair_orders.reshape(1, PAIRS))
    weights, near = pl.pallas_call(
        pack_kernel,
        out_shape=(
            jax.ShapeDtypeStruct((16, HALF * LANES), BF16),
            jax.ShapeDtypeStruct((16, CYCLES // 2 + CYCLES), F32),
        ),
        in_specs=[VMEM, VMEM, HBM, HBM],
        out_specs=(VMEM, VMEM),
        scratch_shapes=[
            pltpu.VMEM((COLS + HALF, 8, LANES), F32),
            pltpu.VMEM((HALF * LANES, CYCLES // 2), BF16),
            pltpu.VMEM((HALF * LANES, CYCLES), BF16),
            pltpu.SemaphoreType.DMA((2, PARTS)),
        ],
        compiler_params=params(52),
        cost_estimate=pl.CostEstimate(flops=30_000_000_000, bytes_accessed=4_000_000, transcendentals=0),
        name="pack",
    )(cycles, got.reshape(2 * PAIRS, LANES), own, derivative[0, 0])
    spectra = pl.pallas_call(
        sums_kernel,
        out_shape=jax.ShapeDtypeStruct((2 * PAIRS, LANES), F32),
        in_specs=[VMEM] * 4,
        out_specs=VMEM,
        scratch_shapes=[pltpu.VMEM((LANES, CYCLES), F32), pltpu.VMEM((CYCLES, LANES), F32)],
        compiler_params=params(8),
        name="sums",
    )(cycles, weights, near, other)
    pieces = lax.all_to_all(
        spectra.reshape(2 * PAIRS, 1, LANES), ("band", "shard"), 0, 0,
        axis_index_groups=[[PAIRS * b + s for b in range(2) for s in shards]], tiled=True,
    )
    fields = pl.pallas_call(
        field_kernel,
        out_shape=jax.ShapeDtypeStruct((3, 2, NLON), F32),
        in_specs=[VMEM, VMEM, VMEM],
        out_specs=HBM,
        scratch_shapes=[
            pltpu.VMEM((8 * TURNS, 4 * PAIRS), BF16),
            *[pltpu.VMEM((3, 2, min(STEP * INNER, NLON - n * INNER)), F32) for n in range(0, TURNS, STEP)],
            pltpu.SemaphoreType.DMA((TURNS // STEP,)),
        ],
        compiler_params=params(8),
        name="fields",
    )(pieces.reshape(2 * PAIRS, LANES), lon, turns)
    return fields.transpose(1, 0, 2)


def solution(mesh):
    placed = (
        P(None, None, "shard"),
        P(),
        P("shard", "band", "comp"),
        P("comp", "shard", "band", None),
    )
    return jax.shard_map(
        on_device,
        mesh=mesh,
        in_specs=placed,
        out_specs=P(("shard", "band"), "comp", None),
        check_vma=False,
    )
```

```python
import functools

import jax
import jax.numpy as jnp
from jax import lax
from jax.experimental import pallas as pl
from jax.experimental.pallas import tpu as pltpu
from jax.sharding import PartitionSpec as P

DEGS = 5120
NLON = 21600
PAIRS = 128
CYCLES = 512
SPAN = 40
LANES = 128
COLS = DEGS // LANES
HALF = COLS // 2
INNER = 256
OUTER = -(-NLON // INNER)
TURNS = 88
PARTS = 10
PART = HALF * LANES // PARTS
STEP = 22
FIRST = 76
F32 = jnp.float32
BF16 = jnp.bfloat16
VMEM = pl.BlockSpec(memory_space=pltpu.VMEM)
HBM = pl.BlockSpec(memory_space=pltpu.HBM)


def params(mib):
    return pltpu.CompilerParams(vmem_limit_bytes=mib * 2**20)


def iota(shape, axis):
    return lax.broadcasted_iota(jnp.int32, shape, axis)


def send_kernel(coef_ref, out_ref, lines_ref, sems):
    shard = lax.axis_index("shard")
    lines_ref[...] = jnp.zeros_like(lines_ref)
    copies = []
    for k in range(2):
        for g in range(0, SPAN, 8):
            start = pl.multiple_of(lax.rem(shard * SPAN + (64 * k + g), LANES), 8)
            copies.append(
                pltpu.make_async_copy(
                    coef_ref.at[k, pl.ds(g, 8), :], lines_ref.at[pl.ds(start, 8), :], sems.at[k, g // 8]
                )
            )
            copies[-1].start()
    for copy in copies:
        copy.wait()
    rows = lines_ref[...].T
    out_ref[pl.ds(0, 2 * (PAIRS - FIRST)), :] = rows[2 * FIRST :]
    out_ref[pl.ds(2 * (PAIRS - FIRST), 2 * FIRST), :] = rows[: 2 * FIRST]


def turn(phase):
    rest = wrap(phase)
    half = rest * (jnp.pi / NLON)
    square = half * half
    sine = jnp.full_like(half, -1.0 / 39916800.0)
    for c in (1.0 / 362880.0, -1.0 / 5040.0, 1.0 / 120.0, -1.0 / 6.0, 1.0):
        sine = sine * square + c
    sine = sine * half
    cosine = jnp.full_like(half, 1.0 / 479001600.0)
    for c in (-1.0 / 3628800.0, 1.0 / 40320.0, -1.0 / 720.0, 1.0 / 24.0, -0.5, 1.0):
        cosine = cosine * square + c
    return 1.0 - 2.0 * sine * sine, 2.0 * sine * cosine


def wrap(phase):
    return phase - jnp.round(phase * (1.0 / NLON)) * NLON


def table_kernel(orders_ref, lon_ref, turns_ref, cycles_ref):
    low = orders_ref[...].astype(F32)
    for j in range(2):
        order = low if j == 0 else DEGS - low
        inner = iota((INNER, PAIRS), 0).astype(F32)
        cosine, sine = turn(inner * order)
        lon_ref[:, pl.ds(j * PAIRS, PAIRS)] = cosine.astype(BF16)
        lon_ref[:, pl.ds((2 + j) * PAIRS, PAIRS)] = sine.astype(BF16)
        outer = iota((TURNS, PAIRS), 0).astype(F32)
        cosine, sine = turn(wrap(outer * order) * INNER)
        turns_ref[pl.ds(0, TURNS), pl.ds(j * PAIRS, PAIRS)] = cosine
        turns_ref[pl.ds(TURNS, TURNS), pl.ds(j * PAIRS, PAIRS)] = sine
    offset = (iota((8, CYCLES), 1).astype(F32) + (0.5 - CYCLES / 2)) * (jnp.pi / (2 * CYCLES))
    square = offset * offset
    sine = jnp.full_like(offset, 1.0 / 40320.0)
    for c in (-1.0 / 720.0, 1.0 / 24.0, -0.5, 1.0):
        sine = sine * square + c
    cosine = jnp.full_like(offset, 1.0 / 362880.0)
    for c in (-1.0 / 5040.0, 1.0 / 120.0, -1.0 / 6.0, 1.0):
        cosine = cosine * square + c
    row = iota((8, CYCLES), 0)
    own = jnp.sum(jnp.where(iota((1, PAIRS), 1) == lax.axis_index("shard"), low, 0.0), axis=1, keepdims=True)
    factor = jnp.where((row & 1) == 0, own, DEGS - own) / DEGS
    factor = jnp.where(row < 6, factor, -factor)
    cycles_ref[pl.ds(0, 8), :] = jnp.where(row < 4, -cosine * offset, factor) / sine
    cycles_ref[pl.ds(8, 8), :] = jnp.broadcast_to(own, (8, CYCLES))


def pack_kernel(cycles_ref, got_ref, own_any, deriv_any, weight_ref, near_ref, flat_ref, own_ref, deriv_ref, sems):
    copies = []
    for c in range(PARTS):
        rows = pl.ds(c * PART, PART)
        copies.append(
            (
                pltpu.make_async_copy(own_any.at[rows, :], own_ref.at[rows, :], sems.at[0, c]),
                pltpu.make_async_copy(deriv_any.at[rows, :], deriv_ref.at[rows, :], sems.at[1, c]),
            )
        )
        for copy in copies[-1]:
            copy.start()
    group_zero = lax.axis_index("comp") == 0
    band = lax.axis_index("band")
    order = jnp.max(cycles_ref[8:16, 0:LANES]).astype(jnp.int32)
    lane = iota((8, LANES), 1)
    row = iota((8, LANES), 0)
    upper = row < 4
    columns = [None] * COLS
    on_cos = (row & 2) == 0
    for w in range(DEGS // SPAN // 4):
        four = got_ref[pl.ds(2 * ((4 * w - FIRST) % PAIRS), 8), :]
        moved = pltpu.roll(four, 64, 1)
        turned = [(pltpu.roll(four, 2 * a, 0) if a else four) for a in range(4)]
        turned_sin = [(pltpu.roll(moved, 2 * a, 0) if a else moved) for a in range(4)]
        mixed = [jnp.where(on_cos, turned[a], turned_sin[(a + 1) % 4]) for a in range(4)]
        for t in range(4):
            piece = jnp.where(upper, mixed[-t % 4], mixed[(2 - t) % 4])
            first = SPAN * (4 * w + t)
            for v in range(first // LANES, (first + SPAN - 1) // LANES + 1):
                if columns[v] is None:
                    columns[v] = piece
                else:
                    columns[v] = jnp.where(lane >= first - LANES * v, piece, columns[v])
    for v in range(COLS):
        flat_ref[v] = columns[v]
    flat_ref[pl.ds(COLS, HALF)] = jnp.zeros((HALF, 8, LANES), F32)
    chunk = order // LANES
    rest = order - chunk * LANES
    back = lax.rem(LANES - rest, LANES)
    second_order = (row & 1) == 1
    for v in range(HALF):
        low = pltpu.roll(flat_ref[HALF * band + chunk + v], back, 1)
        high = pltpu.roll(flat_ref[jnp.minimum(HALF * band + chunk + v + 1, COLS + HALF - 1)], back, 1)
        lead = jnp.where(lane < LANES - rest, low, high)
        tail = flat_ref[HALF * band + v]
        position = (HALF * band + v) * LANES + lane
        inside = position < DEGS - order
        value = jnp.where(inside == second_order, 0.0, jnp.where(second_order, tail, lead))
        degree = jnp.where(inside, position + order, position).astype(F32)
        linear = (degree + 1.0) / DEGS
        shifted = (degree + 2.0) / DEGS
        on_values = jnp.where(group_zero, jnp.where(upper, linear * shifted, linear), jnp.where(upper, shifted, 0.0))
        on_deriv = jnp.where(upper, jnp.where(group_zero, 0.0, shifted), 1.0)
        both = jnp.concatenate([on_values * value, on_deriv * value], axis=0)
        weight_ref[:, pl.ds(v * LANES, LANES)] = both.astype(BF16)
    from_own = jnp.zeros((16, CYCLES // 2), F32)
    from_deriv = jnp.zeros((16, CYCLES), F32)
    for c in range(PARTS):
        for copy in copies[c]:
            copy.wait()
        rows = pl.ds(c * PART, PART)
        weights = weight_ref[:, rows]
        from_own += jnp.dot(weights, own_ref[rows, :], preferred_element_type=F32)
        from_deriv += jnp.dot(weights, deriv_ref[rows, :], preferred_element_type=F32)
    near_ref[:, pl.ds(0, CYCLES // 2)] = from_own
    near_ref[:, pl.ds(CYCLES // 2, CYCLES)] = from_deriv


def sums_kernel(cycles_ref, weight_ref, near_ref, other_ref, out_ref, spec_ref, turned_ref):
    group_zero = lax.axis_index("comp") == 0
    from_own = near_ref[:, : CYCLES // 2]
    from_deriv = near_ref[:, CYCLES // 2 :]
    from_other = jnp.dot(weight_ref[...], other_ref[...], preferred_element_type=F32)
    from_values = jnp.concatenate(
        [jnp.where(group_zero, from_own, from_other), jnp.where(group_zero, from_other, from_own)], axis=1
    )
    zero = from_values[0:4]
    one = from_values[4:8] + from_deriv[8:12]
    two = from_deriv[12:16]
    cotangent = cycles_ref[0:4]
    factor = cycles_ref[4:8]
    along = two - one

    def crossed(x):
        return factor * jnp.concatenate([x[2:4], x[0:2]], axis=0)

    parts = (
        jnp.where(group_zero, along, one + cotangent * zero),
        jnp.where(group_zero, -along - zero, crossed(zero)),
        jnp.where(group_zero, zero, crossed(two)),
    )
    spec_ref[...] = jnp.zeros_like(spec_ref)
    for c in range(3):
        for part in range(4):
            spec_ref[pl.ds(8 * part + 2 * c, 1), :] = parts[c][part : part + 1]
    turned_ref[...] = spec_ref[...].T
    for b in range(2):
        for first, count, place in ((FIRST, PAIRS - FIRST, 0), (0, FIRST, PAIRS - FIRST)):
            even = turned_ref[pl.ds(4 * first + 2 * b, count, stride=4), :]
            odd = turned_ref[pl.ds(4 * first + 2 * b + 1, count, stride=4), :]
            out_ref[pl.ds(b * PAIRS + place, count), :] = even + pltpu.roll(odd, 1, 1)


def field_kernel(got_ref, lon_ref, turns_ref, out_ref, left_ref, *rest):
    parts, sems = rest[:-1], rest[-1]
    summed = got_ref[pl.ds(0, PAIRS), :] + got_ref[pl.ds(PAIRS, PAIRS), :]
    rows = pltpu.roll(summed.T, FIRST, 1)
    cos_part = jnp.concatenate([rows[0:8], rows[8:16]], axis=1)
    sin_part = jnp.concatenate([rows[16:24], rows[24:32]], axis=1)
    lon = lon_ref[...]
    copies = []
    for i, part_ref in enumerate(parts):
        first = STEP * i
        for n in range(first, first + STEP, 2):
            halves = []
            for d in range(2):
                turn_cos = turns_ref[pl.ds(n + d, 1), :]
                turn_sin = turns_ref[pl.ds(TURNS + n + d, 1), :]
                halves.append(
                    jnp.concatenate(
                        [cos_part * turn_cos + sin_part * turn_sin, sin_part * turn_cos - cos_part * turn_sin], axis=1
                    )
                )
            left_ref[pl.ds(8 * n, 16), :] = jnp.concatenate(halves, axis=0).astype(BF16)
        field = lax.dot_general(
            left_ref[pl.ds(8 * first, 8 * STEP), :], lon, (((1,), (1,)), ((), ())), preferred_element_type=F32
        )
        for d in range(STEP):
            width = min(INNER, NLON - (first + d) * INNER)
            if width <= 0:
                continue
            for c in range(3):
                part_ref[c, :, pl.ds(d * INNER, width)] = field[8 * d + 2 * c : 8 * d + 2 * c + 2, :width]
        width = part_ref.shape[2]
        copies.append(pltpu.make_async_copy(part_ref, out_ref.at[:, :, pl.ds(first * INNER, width)], sems.at[i]))
        copies[-1].start()
    for copy in copies:
        copy.wait()


def on_device(coefficients, pair_orders, legendre, derivative):
    sent = pl.pallas_call(
        send_kernel,
        out_shape=jax.ShapeDtypeStruct((2 * PAIRS, LANES), F32),
        in_specs=[HBM],
        out_specs=VMEM,
        scratch_shapes=[pltpu.VMEM((LANES, 2 * PAIRS), F32), pltpu.SemaphoreType.DMA((2, SPAN // 8))],
        compiler_params=params(60),
        name="send",
    )(coefficients.transpose(0, 2, 1))
    sent, own = lax.optimization_barrier((sent, legendre[0]))
    shards = [(FIRST + i) % PAIRS for i in range(PAIRS)]
    got = lax.all_to_all(
        sent.reshape(PAIRS, 2, LANES), "shard", 0, 0, axis_index_groups=[shards], tiled=True
    )
    other = lax.ppermute(own, "comp", [(0, 1), (1, 0)])
    lon, turns, cycles = pl.pallas_call(
        table_kernel,
        out_shape=(
            jax.ShapeDtypeStruct((INNER, 4 * PAIRS), BF16),
            jax.ShapeDtypeStruct((2 * TURNS, 2 * PAIRS), F32),
            jax.ShapeDtypeStruct((16, CYCLES), F32),
        ),
        in_specs=[VMEM],
        out_specs=(VMEM, VMEM, VMEM),
        compiler_params=params(4),
        cost_estimate=pl.CostEstimate(flops=400_000_000, bytes_accessed=600_000, transcendentals=0),
        name="tables",
    )(pair_orders.reshape(1, PAIRS))
    weights, near = pl.pallas_call(
        pack_kernel,
        out_shape=(
            jax.ShapeDtypeStruct((16, HALF * LANES), BF16),
            jax.ShapeDtypeStruct((16, CYCLES // 2 + CYCLES), F32),
        ),
        in_specs=[VMEM, VMEM, HBM, HBM],
        out_specs=(VMEM, VMEM),
        scratch_shapes=[
            pltpu.VMEM((COLS + HALF, 8, LANES), F32),
            pltpu.VMEM((HALF * LANES, CYCLES // 2), BF16),
            pltpu.VMEM((HALF * LANES, CYCLES), BF16),
            pltpu.SemaphoreType.DMA((2, PARTS)),
        ],
        compiler_params=params(52),
        cost_estimate=pl.CostEstimate(flops=30_000_000_000, bytes_accessed=4_000_000, transcendentals=0),
        name="pack",
    )(cycles, got.reshape(2 * PAIRS, LANES), own, derivative[0, 0])
    spectra = pl.pallas_call(
        sums_kernel,
        out_shape=jax.ShapeDtypeStruct((2 * PAIRS, LANES), F32),
        in_specs=[VMEM] * 4,
        out_specs=VMEM,
        scratch_shapes=[pltpu.VMEM((LANES, CYCLES), F32), pltpu.VMEM((CYCLES, LANES), F32)],
        compiler_params=params(8),
        name="sums",
    )(cycles, weights, near, other)
    pieces = lax.all_to_all(
        spectra.reshape(2 * PAIRS, 1, LANES), ("band", "shard"), 0, 0,
        axis_index_groups=[[PAIRS * b + s for b in range(2) for s in shards]], tiled=True,
    )
    fields = pl.pallas_call(
        field_kernel,
        out_shape=jax.ShapeDtypeStruct((3, 2, NLON), F32),
        in_specs=[VMEM, VMEM, VMEM],
        out_specs=HBM,
        scratch_shapes=[
            pltpu.VMEM((8 * TURNS, 4 * PAIRS), BF16),
            *[pltpu.VMEM((3, 2, min(STEP * INNER, NLON - n * INNER)), F32) for n in range(0, TURNS, STEP)],
            pltpu.SemaphoreType.DMA((TURNS // STEP,)),
        ],
        compiler_params=params(8),
        name="fields",
    )(pieces.reshape(2 * PAIRS, LANES), lon, turns)
    return fields.transpose(1, 0, 2)


def solution(mesh):
    placed = (
        P(None, None, "shard"),
        P(),
        P("shard", "band", "comp"),
        P("comp", "shard", "band", None),
    )
    return jax.shard_map(
        on_device,
        mesh=mesh,
        in_specs=placed,
        out_specs=P(("shard", "band"), "comp", None),
        check_vma=False,
    )
```
